512 devices in a mesh: row: 32 (over z, x), col: 16 (over y, core).
Axes of the slice: x: 4, y: 8, z: 8, core: 2. Of those that a mesh axis runs over, the one named last changes fastest.
Arguments:
- vectors: bfloat16 [64, 262144], P(None, ('row', 'col')), may hold values from -6 to 6
- tiles: bfloat16 [12288, 256, 256], P(('row', 'col')), may hold values from -0.125 to 0.125
- tile_row: int32 [12288], P(('row', 'col')), may hold values from 0 to 31
- tile_col: int32 [12288], P(('row', 'col')), may hold values from 0 to 63
- tile_count: int32 [512], P(('row', 'col')), may hold values from 1 to 24, 7680 in all
- lower: float32 [1], replicated, may hold values from -1.5 to -0.5
- upper: float32 [1], replicated, may hold values from 0.5 to 1.5
Outputs:
- filtered: bfloat16 [64, 262144], P(None, ('row', 'col'))
The draws below stay inside these ranges and needn't reach their ends.
Inputs may be any that keep to these rules, and one draw needn't show every extreme that they name: `tile_row`: block rows of a slot inside its device's row panel. `tile_col`: block columns of a slot inside its device's column panel. `tile_count`: slots past a device's count are ignored; some device uses all 24 slots.
All inputs are finite; a program needn't handle non-finite values.
Results may differ from the reference program's by a relative error of at most 0.023.
Values may be sent and summed in bfloat16 or wider, within the bound.
No kernel may reach another device: no remote copies, remote signals or barrier semaphores. Data moves between devices by JAX's collectives and lax.ppermute only.
A program may use at most 64 MiB of HBM per device.

```python
import math
import jax
import jax.numpy as jnp
import numpy as np
from jax import lax

N = 262144
TB = 256
NV = 64
TILES_DEV = 24
DEGREE = 2
NB = 1024
BR = 32
BC = 64
SLOTS = 12288
N_ROW = 32
N_COL = 16
DEVICES = 512


def set_ends(values, key, smallest, high):
    index_at = [jax.random.randint(jax.random.fold_in(key, axis), (), 0, length) for axis, length in enumerate(values.shape)]
    widest = values.shape.index(max(values.shape))
    next_to = index_at[:widest] + [(index_at[widest] + 1) % values.shape[widest]] + index_at[widest + 1:]
    return values.at[tuple(index_at)].set(smallest).at[tuple(next_to)].set(high)


def steps_of(own_key, extent, split, smallest, high):
    level = 1.0
    for position, shards_of in split:
        draws = jax.random.uniform(jax.random.fold_in(jax.random.fold_in(own_key, 6), position), (shards_of,), jnp.float32, smallest / len(split), high / len(split))
        level = level * jnp.repeat(jnp.exp(draws), extent[position] // shards_of).reshape((-1,) + (1,) * (len(extent) - 1 - position))
    return level


def profile(count, total, reach, slope):
    portions = [(1 << 20) // math.isqrt(rank ** slope) + 1 for rank in range(2, count + 1)]
    surplus, given = total - reach - (count - 1), [1] * (count - 1)
    while surplus > 0:
        candidates = [i for i in range(count - 1) if given[i] < reach]
        whole, remaining = sum([portions[i] for i in candidates]), surplus
        for i in candidates:
            addition = min(reach - given[i], max(1, remaining * portions[i] // whole), surplus)
            given[i] = given[i] + addition
            surplus = surplus - addition
    return np.array([reach] + given)


def ragged(key, count, total, most, skew):
    if count == 2:
        one = jax.random.randint(key, (), max(1, total - most), min(most, total - 1) + 1)
        return jnp.stack([one, total - one])
    lengths = jnp.asarray(profile(count, total, most, skew), jnp.int32)
    twos = (count - 1) // 2
    giver, sink = lengths[1:1 + 2 * twos:2], lengths[2:2 + 2 * twos:2]
    slack = jnp.minimum(giver - 1, most - sink)
    moved = jax.random.randint(jax.random.fold_in(key, 1), (twos,), 0, 1 << 20) % (slack + 1)
    lengths = lengths.at[1:1 + 2 * twos:2].set(giver - moved).at[2:2 + 2 * twos:2].set(sink + moved)
    return lengths[jax.random.permutation(jax.random.fold_in(key, 2), count)]


def noise(key, extent, scale, limit, split=(), kind=jnp.bfloat16):
    entries = scale * jax.random.normal(key, extent, jnp.float32)
    if split:
        entries = entries * steps_of(key, extent, split, -0.22, 0.18)
    return jnp.clip(entries, -limit, limit).astype(kind)


def setup_inputs(seed: int = 0) -> dict:
    key_list = jax.random.split(jax.random.key(seed), 8)
    vectors = noise(key_list[0], (NV, N), 1.0, 6.0, ((1, 512),))
    tiles = noise(key_list[1], (SLOTS, TB, TB), (TB * max(1, TILES_DEV * N_COL * 5 // (8 * BR))) ** -0.5, 0.125, ((0, 512),))
    tile_row = set_ends(jax.random.randint(key_list[2], (SLOTS,), 0, BR), jax.random.fold_in(key_list[2], 1), 0, BR - 1).astype(jnp.int32)
    tile_col = set_ends(jax.random.randint(key_list[3], (SLOTS,), 0, BC), jax.random.fold_in(key_list[3], 1), 0, BC - 1).astype(jnp.int32)
    tile_count = ragged(key_list[4], DEVICES, DEVICES * TILES_DEV * 5 // 8, TILES_DEV, 2).astype(jnp.int32)
    lower = jnp.clip(jax.random.uniform(key_list[5], (1,), jnp.float32, -1.5, -0.5), -1.5, -0.5)
    upper = jnp.clip(jax.random.uniform(key_list[6], (1,), jnp.float32, 0.5, 1.5), 0.5, 1.5)
    return {"vectors": vectors, "tiles": tiles, "tile_row": tile_row, "tile_col": tile_col, "tile_count": tile_count, "lower": lower, "upper": upper}


def apply_matrix(block, tiles, tile_row, tile_col, tile_count):
    blocks = block.reshape(NV, NB, TB)
    total = jnp.zeros((N_ROW, NV, BR * TB), jnp.float32)

    def per_device(d, total):
        start = d * TILES_DEV
        local = lax.dynamic_slice_in_dim(tiles, start, TILES_DEV, 0)
        rows = lax.dynamic_slice_in_dim(tile_row, start, TILES_DEV, 0)
        cols = lax.dynamic_slice_in_dim(tile_col, start, TILES_DEV, 0)
        grid_row = d // N_COL
        grid_col = d % N_COL
        picked = jnp.take(blocks, (grid_col * BC + cols).astype(jnp.int32), axis=1).astype(jnp.float32)
        prod = jnp.einsum("vtk,tjk->tvj", picked, local.astype(jnp.float32))
        live = (jnp.arange(TILES_DEV, dtype=jnp.int32) < tile_count[d]).astype(jnp.float32)
        onehot = (rows[None, :] == jnp.arange(BR, dtype=jnp.int32)[:, None]).astype(jnp.float32) * live[None, :]
        part = jnp.einsum("bt,tvj->vbj", onehot, prod, precision=lax.Precision.HIGHEST)
        part = part.reshape(NV, BR * TB).astype(jnp.bfloat16).astype(jnp.float32)
        return total.at[grid_row].add(part)

    total = lax.fori_loop(0, DEVICES, per_device, total)
    return jnp.transpose(total, (1, 0, 2)).reshape(NV, N)


def reference(vectors, tiles, tile_row, tile_col, tile_count, lower, upper):
    center = (upper[0] + lower[0]) / 2.0
    half = (upper[0] - lower[0]) / 2.0
    previous = vectors
    current = vectors
    for step in range(DEGREE):
        sums = apply_matrix(current, tiles, tile_row, tile_col, tile_count)
        shifted = (sums - center * current.astype(jnp.float32)) / half
        if step == 0:
            following = shifted
        else:
            following = 2.0 * shifted - previous.astype(jnp.float32)
        previous, current = current, following.astype(jnp.bfloat16)
    return current
```

```python
import functools

import jax
import jax.numpy as jnp
from jax import lax
from jax.experimental import pallas as pl
from jax.experimental.pallas import tpu as pltpu
from jax.sharding import PartitionSpec as P

NZ, NX, NY, NC = 8, 4, 8, 2
TB = 256
NV = 64
SLOTS = 24
BR = 32
DEGREE = 2
PIECE = 2 * TB
AXES = ("row", "col")

PLACES = [(z, x, y, c) for z in range(NZ) for x in range(NX) for y in range(NY) for c in range(NC)]


def number(z, x, y, c):
    return (((z % NZ) * NX + x % NX) * NY + y % NY) * NC + c % NC


def permute(value, move):
    return lax.ppermute(value, AXES, [(number(*p), number(*move(*p))) for p in PLACES])


def grouped(key):
    groups = {}
    for place in PLACES:
        groups.setdefault(key(*place), []).append(number(*place))
    return [sorted(group) for group in groups.values()]


def exchange(value, groups):
    return lax.all_to_all(value, AXES, 0, 0, axis_index_groups=groups, tiled=True)


def class_of(z, x, c):
    return (z + 2 * x) % 4 if c == 0 else (x + 2 * z) % 4


CLASSES = grouped(lambda z, x, y, c: (y, c, class_of(z, x, c)))
LINES = grouped(lambda z, x, y, c: (z, x, c))


def to_column_plane(z, x, y, c):
    return (y, (x % 2) * 2 + c, z, x // 2)


def along(sign):
    return lambda z, x, y, c: (z + sign, x, y, c) if c == 0 else (z, x + sign, y, c)


def across(sign):
    return lambda z, x, y, c: (z, x + sign, y, c) if c == 0 else (z + sign, x, y, c)


def other_core(z, x, y, c):
    return (z, x, y, 1 - c)


def column_panel(piece):
    mine = permute(piece, to_column_plane)
    bundle = exchange(jnp.broadcast_to(mine[None], (8,) + mine.shape), CLASSES)
    below = permute(bundle, along(1))
    above = permute(bundle, along(-1))
    first = permute(bundle[:4], across(1))
    second = permute(bundle[4:], across(-1))
    return bundle, below, above, first, second


def block_places(tile_col, z, x, c):
    from_z = (tile_col % 32) // 4
    from_x = (tile_col // 32) * 2 + (tile_col // 2) % 2
    theirs = jnp.where(c == 0, from_z + 2 * from_x, from_x + 2 * from_z)
    own = jnp.where(c == 0, z + 2 * x, x + 2 * z)
    member = jnp.where(c == 0, (from_z // 2) * 2 + from_x // 2, from_z)
    apart = (theirs - own) % 4
    start = jnp.where(apart == 0, 0, jnp.where(apart == 3, 8, jnp.where(apart == 1, 16, 24)))
    return (start + member) * 2 + tile_col % 2


def product_kernel(
    place_ref, row_ref, core_ref, b0, b1, b2, b3, b4, tiles_hbm,
    keep_ref, give_ref, panel, tiles, total, panel_sems, tile_sems,
):
    chunk = SLOTS // 4
    loads = []
    for index, (source, start, size) in enumerate(
        ((b0, 0, 8), (b1, 8, 8), (b2, 16, 8), (b3, 24, 4), (b4, 28, 4))
    ):
        loads.append(
            pltpu.make_async_copy(source, panel.at[pl.ds(start, size)], panel_sems.at[index])
        )
    tile_loads = []
    for index in range(4):
        part = pl.ds(index * chunk, chunk)
        tile_loads.append(
            pltpu.make_async_copy(tiles_hbm.at[part], tiles.at[part], tile_sems.at[index])
        )
    for load in loads + tile_loads:
        load.start()
    total[...] = jnp.zeros_like(total)
    for load in loads:
        load.wait()
    for index in range(4):
        tile_loads[index].wait()
        slots = range(index * chunk, (index + 1) * chunk)
        products = []
        for slot in slots:
            place = place_ref[slot]
            half = pl.multiple_of((place % 2) * TB, TB)
            block = panel[place // 2, :, pl.ds(half, TB)]
            products.append(
                lax.dot_general(
                    block, tiles[slot], (((1,), (1,)), ((), ())),
                    preferred_element_type=jnp.float32,
                )
            )
        for slot, product in zip(slots, products):
            row = row_ref[slot]
            total[row] = total[row] + product
    core = core_ref[0]
    for line in range(NY):
        for half in range(2):
            columns = slice(half * TB, (half + 1) * TB)
            keep_ref[line, :, columns] = total[4 * line + 2 * core + half].astype(jnp.bfloat16)
            give_ref[line, :, columns] = total[4 * line + 2 * (1 - core) + half].astype(jnp.bfloat16)


def local_product(parts, tiles, places, rows, core):
    half_panel = jax.ShapeDtypeStruct((NY, NV, PIECE), jnp.bfloat16)
    return pl.pallas_call(
        product_kernel,
        out_shape=(half_panel, half_panel),
        in_specs=[pl.BlockSpec(memory_space=pltpu.SMEM)] * 3
        + [pl.BlockSpec(memory_space=pl.ANY)] * 6,
        out_specs=(pl.BlockSpec(memory_space=pltpu.VMEM),) * 2,
        scratch_shapes=[
            pltpu.VMEM((32, NV, PIECE), jnp.bfloat16),
            pltpu.VMEM((SLOTS, TB, TB), jnp.bfloat16),
            pltpu.VMEM((BR + 1, NV, TB), jnp.float32),
            pltpu.SemaphoreType.DMA((5,)),
            pltpu.SemaphoreType.DMA((4,)),
        ],
        compiler_params=pltpu.CompilerParams(vmem_limit_bytes=24 * 1024 * 1024),
        cost_estimate=pl.CostEstimate(
            flops=2 * SLOTS * NV * TB * TB, bytes_accessed=8 * 1024 * 1024, transcendentals=0
        ),
        name="block_products",
    )(places, rows, core, *parts, tiles)


def recurrence(sums, current, previous, center, half, step):
    shifted = (sums - center * current.astype(jnp.float32)) / half
    if step == 0:
        return shifted.astype(jnp.bfloat16)
    return (2.0 * shifted - previous.astype(jnp.float32)).astype(jnp.bfloat16)


def on_device(vectors, tiles, tile_row, tile_col, tile_count, lower, upper):
    center = (upper[0] + lower[0]) / 2.0
    half = (upper[0] - lower[0]) / 2.0
    row, col = lax.axis_index("row"), lax.axis_index("col")
    z, x, core = row // NX, row % NX, col % NC
    places = block_places(tile_col, z, x, core)
    used = jnp.arange(SLOTS, dtype=jnp.int32) < tile_count[0]
    rows = jnp.where(used, tile_row, BR)
    core_ref = core.astype(jnp.int32)[None]
    current = previous = vectors
    for step in range(DEGREE):
        parts = column_panel(current)
        keep, give = local_product(parts, tiles, places, rows, core_ref)
        taken = permute(give, other_core)
        pair = (keep.astype(jnp.float32) + taken.astype(jnp.float32)).astype(jnp.bfloat16)
        sums = jnp.sum(exchange(pair, LINES).astype(jnp.float32), axis=0)
        following = recurrence(sums, current, previous, center, half, step)
        previous, current = (current, following)
    return current


def solution(mesh):
    return jax.shard_map(
        on_device,
        mesh=mesh,
        in_specs=(
            P(None, AXES),
            P(AXES, None, None),
            P(AXES),
            P(AXES),
            P(AXES),
            P(),
            P(),
        ),
        out_specs=P(None, AXES),
        check_vma=False,
    )
```

```python
import functools

import jax
import jax.numpy as jnp
from jax import lax
from jax.experimental import pallas as pl
from jax.experimental.pallas import tpu as pltpu
from jax.sharding import PartitionSpec as P

NZ, NX, NY, NC = 8, 4, 8, 2
TB = 256
NV = 64
SLOTS = 24
BR = 32
DEGREE = 2
PIECE = 2 * TB
AXES = ("row", "col")

PLACES = [(z, x, y, c) for z in range(NZ) for x in range(NX) for y in range(NY) for c in range(NC)]


def number(z, x, y, c):
    return (((z % NZ) * NX + x % NX) * NY + y % NY) * NC + c % NC


def permute(value, move):
    return lax.ppermute(value, AXES, [(number(*p), number(*move(*p))) for p in PLACES])


def grouped(key):
    groups = {}
    for place in PLACES:
        groups.setdefault(key(*place), []).append(number(*place))
    return [sorted(group) for group in groups.values()]


def exchange(value, groups):
    return lax.all_to_all(value, AXES, 0, 0, axis_index_groups=groups, tiled=True)


def class_of(z, x, c):
    return (z + 2 * x) % 4 if c == 0 else (x + 2 * z) % 4


CLASSES = grouped(lambda z, x, y, c: (y, c, class_of(z, x, c)))
LINES = grouped(lambda z, x, y, c: (z, x, c))


def to_column_plane(z, x, y, c):
    return (2 * z + 4 - y, x if c == 0 else 3 - x, z, x // 2)


def along(sign):
    return lambda z, x, y, c: (z + sign, x, y, c) if c == 0 else (z, x + sign, y, c)


def across(sign):
    return lambda z, x, y, c: (z, x + sign, y, c) if c == 0 else (z + sign, x, y, c)


def other_core(z, x, y, c):
    return (z, x, y, 1 - c)


def column_panel(mine):
    bundle = exchange(jnp.broadcast_to(mine[None], (8,) + mine.shape), CLASSES)
    below = permute(bundle, along(1))
    above = permute(bundle, along(-1))
    beside = permute(bundle, across(1))
    return bundle, below, above, beside


def block_places(tile_col, z, x, y, c):
    owner_x = 2 * c + tile_col // 32
    from_z = (2 * y + 4 - (tile_col % 32) // 4) % 8
    from_x = jnp.where((tile_col // 2) % 2 == 0, owner_x, 3 - owner_x)
    theirs = jnp.where(c == 0, from_z + 2 * from_x, from_x + 2 * from_z)
    own = jnp.where(c == 0, z + 2 * x, x + 2 * z)
    member = jnp.where(c == 0, (from_z // 2) * 2 + from_x // 2, from_z)
    apart = (theirs - own) % 4
    start = jnp.where(apart == 0, 0, jnp.where(apart == 3, 8, jnp.where(apart == 1, 16, 24)))
    return (start + member) * 2 + tile_col % 2


def load_kernel(tiles_hbm, tiles_ref, sem):
    load = pltpu.make_async_copy(tiles_hbm, tiles_ref, sem)
    load.start()
    load.wait()


def load_tiles(tiles):
    return pl.pallas_call(
        load_kernel,
        out_shape=jax.ShapeDtypeStruct(tiles.shape, tiles.dtype),
        in_specs=[pl.BlockSpec(memory_space=pl.ANY)],
        out_specs=pl.BlockSpec(memory_space=pl.ANY),
        scratch_shapes=[pltpu.SemaphoreType.DMA],
        compiler_params=pltpu.CompilerParams(vmem_limit_bytes=16 * 1024 * 1024),
        name="load_tiles",
    )(tiles)


def product_kernel(
    place_ref, row_ref, core_ref, b0, b1, b2, b3, tiles, keep_ref, give_ref, total
):
    total[...] = jnp.zeros_like(total)
    chunk = 6
    for first in range(0, SLOTS, chunk):
        slots = range(first, first + chunk)
        products = []
        for slot in slots:
            place = place_ref[slot]
            part = place // 16
            member = (place // 2) % 8
            columns = pl.ds(pl.multiple_of((place % 2) * TB, TB), TB)
            block = jnp.where(
                part < 2,
                jnp.where(part == 0, b0[member, :, columns], b1[member, :, columns]),
                jnp.where(part == 2, b2[member, :, columns], b3[member, :, columns]),
            )
            products.append(
                lax.dot_general(
                    block, tiles[slot], (((1,), (1,)), ((), ())),
                    preferred_element_type=jnp.float32,
                )
            )
        for slot, product in zip(slots, products):
            row = row_ref[slot]
            total[row] = total[row] + product
    core = core_ref[0]
    for line in range(NY):
        for half in range(2):
            columns = slice(half * TB, (half + 1) * TB)
            keep_ref[line, :, columns] = total[4 * line + 2 * core + half].astype(jnp.bfloat16)
            give_ref[line, :, columns] = total[4 * line + 2 * (1 - core) + half].astype(jnp.bfloat16)


def local_product(parts, tiles, places, rows, core):
    half_panel = jax.ShapeDtypeStruct((NY, NV, PIECE), jnp.bfloat16)
    return pl.pallas_call(
        product_kernel,
        out_shape=(half_panel, half_panel),
        in_specs=[pl.BlockSpec(memory_space=pltpu.SMEM)] * 3
        + [pl.BlockSpec(memory_space=pltpu.VMEM)] * 5,
        out_specs=(pl.BlockSpec(memory_space=pltpu.VMEM),) * 2,
        scratch_shapes=[pltpu.VMEM((BR + 1, NV, TB), jnp.float32)],
        compiler_params=pltpu.CompilerParams(vmem_limit_bytes=24 * 1024 * 1024),
        cost_estimate=pl.CostEstimate(
            flops=2 * SLOTS * NV * TB * TB, bytes_accessed=8 * 1024 * 1024, transcendentals=0
        ),
        name="block_products",
    )(places, rows, core, *parts, tiles)


def line_sum(keep, taken):
    pair = (keep.astype(jnp.float32) + taken.astype(jnp.float32)).astype(jnp.bfloat16)
    return jnp.sum(exchange(pair, LINES).astype(jnp.float32), axis=0)


def recurrence(sums, current, previous, center, half, step):
    shifted = (sums - center * current.astype(jnp.float32)) / half
    if step == 0:
        return shifted.astype(jnp.bfloat16)
    return (2.0 * shifted - previous.astype(jnp.float32)).astype(jnp.bfloat16)


def on_device(vectors, tiles, tile_row, tile_col, tile_count, lower, upper):
    center = (upper[0] + lower[0]) / 2.0
    half = (upper[0] - lower[0]) / 2.0
    row, col = lax.axis_index("row"), lax.axis_index("col")
    z, x, y, core = row // NX, row % NX, col // NC, col % NC
    places = block_places(tile_col, z, x, y, core)
    used = jnp.arange(SLOTS, dtype=jnp.int32) < tile_count[0]
    rows = jnp.where(used, tile_row, BR)
    core_ref = core.astype(jnp.int32)[None]
    current = previous = vectors
    moved = permute(current, to_column_plane)
    moved, tiles, places, rows, center, half = lax.optimization_barrier(
        (moved, load_tiles(tiles), places, rows, center, half)
    )
    for step in range(DEGREE):
        if step > 0:
            moved = permute(current, to_column_plane)
        parts = column_panel(moved)
        keep, give = local_product(parts, tiles, places, rows, core_ref)
        taken = permute(give, other_core)
        sums = line_sum(keep, taken)
        following = recurrence(sums, current, previous, center, half, step)
        previous, current = (current, following)
    return current


def solution(mesh):
    return jax.shard_map(
        on_device,
        mesh=mesh,
        in_specs=(
            P(None, AXES),
            P(AXES, None, None),
            P(AXES),
            P(AXES),
            P(AXES),
            P(),
            P(),
        ),
        out_specs=P(None, AXES),
        check_vma=False,
    )
```

```python
import functools

import jax
import jax.numpy as jnp
from jax import lax
from jax.experimental import pallas as pl
from jax.experimental.pallas import tpu as pltpu
from jax.sharding import PartitionSpec as P

NZ, NX, NY, NC = 8, 4, 8, 2
TB = 256
NV = 64
SLOTS = 24
BR = 32
DEGREE = 2
PIECE = 2 * TB
AXES = ("row", "col")

PLACES = [(z, x, y, c) for z in range(NZ) for x in range(NX) for y in range(NY) for c in range(NC)]


def number(z, x, y, c):
    return (((z % NZ) * NX + x % NX) * NY + y % NY) * NC + c % NC


def permute(value, move):
    return lax.ppermute(value, AXES, [(number(*p), number(*move(*p))) for p in PLACES])


def grouped(key):
    groups = {}
    for place in PLACES:
        groups.setdefault(key(*place), []).append(number(*place))
    return [sorted(group) for group in groups.values()]


def exchange(value, groups):
    return lax.all_to_all(value, AXES, 0, 0, axis_index_groups=groups, tiled=True)


def class_of(z, x, c):
    return (z + 2 * x) % 4 if c == 0 else (x + 2 * z) % 4


CLASSES = grouped(lambda z, x, y, c: (y, c, class_of(z, x, c)))
LINES = grouped(lambda z, x, y, c: (z, x, c))


def to_column_plane(z, x, y, c):
    return (2 * z + 4 - y, x if c == 0 else 3 - x, z, x // 2)


def along(sign):
    return lambda z, x, y, c: (z + sign, x, y, c) if c == 0 else (z, x + sign, y, c)


def across(sign):
    return lambda z, x, y, c: (z, x + sign, y, c) if c == 0 else (z + sign, x, y, c)


def other_core(z, x, y, c):
    return (z, x, y, 1 - c)


def column_panel(mine):
    bundle = exchange(jnp.broadcast_to(mine[None], (8,) + mine.shape), CLASSES)
    below = permute(bundle, along(1))
    above = permute(bundle, along(-1))
    beside = permute(bundle, across(1))
    return bundle, below, above, beside


def block_places(tile_col, z, x, y, c):
    owner_x = 2 * c + tile_col // 32
    from_z = (2 * y + 4 - (tile_col % 32) // 4) % 8
    from_x = jnp.where((tile_col // 2) % 2 == 0, owner_x, 3 - owner_x)
    theirs = jnp.where(c == 0, from_z + 2 * from_x, from_x + 2 * from_z)
    own = jnp.where(c == 0, z + 2 * x, x + 2 * z)
    member = jnp.where(c == 0, (from_z // 2) * 2 + from_x // 2, from_z)
    apart = (theirs - own) % 4
    start = jnp.where(apart == 0, 0, jnp.where(apart == 3, 8, jnp.where(apart == 1, 16, 24)))
    return (start + member) * 2 + tile_col % 2


def load_kernel(tiles_hbm, tiles_ref, sem):
    load = pltpu.make_async_copy(tiles_hbm, tiles_ref, sem)
    load.start()
    load.wait()


def load_tiles(tiles):
    return pl.pallas_call(
        load_kernel,
        out_shape=jax.ShapeDtypeStruct(tiles.shape, tiles.dtype),
        in_specs=[pl.BlockSpec(memory_space=pl.ANY)],
        out_specs=pl.BlockSpec(memory_space=pl.ANY),
        scratch_shapes=[pltpu.SemaphoreType.DMA],
        compiler_params=pltpu.CompilerParams(vmem_limit_bytes=16 * 1024 * 1024),
        name="load_tiles",
    )(tiles)


def product(block, tile):
    return lax.dot_general(
        block, tile, (((1,), (1,)), ((), ())), preferred_element_type=jnp.float32
    )


def lane_half(place):
    return pl.ds(pl.multiple_of((place % 2) * TB, TB), TB)


def early_kernel(place_ref, row_ref, own, above, beside, tiles, total):
    total[...] = jnp.zeros_like(total)
    chunk = 6
    for first in range(0, SLOTS, chunk):
        slots = range(first, first + chunk)
        products = []
        for slot in slots:
            place = place_ref[slot]
            part = place // 16
            member = (place // 2) % 8
            columns = lane_half(place)
            block = jnp.where(
                part == 0,
                own[member, :, columns],
                jnp.where(part == 2, above[member, :, columns], beside[member, :, columns]),
            )
            products.append(product(block, tiles[slot]))
        for slot, value in zip(slots, products):
            row = jnp.where(place_ref[slot] // 16 == 1, BR, row_ref[slot])
            total[row] = total[row] + value


def late_kernel(
    place_ref, row_ref, core_ref, before, below, tiles, keep_ref, give_ref, total
):
    for slot in range(SLOTS):
        place = place_ref[slot]
        row = row_ref[slot]

        @pl.when(jnp.logical_and(place // 16 == 1, row < BR))
        def _():
            block = below[(place // 2) % 8, :, lane_half(place)]
            total[row] = total[row] + product(block, tiles[slot])

    core = core_ref[0]
    for line in range(NY):
        for half in range(2):
            columns = slice(half * TB, (half + 1) * TB)
            keep_ref[line, :, columns] = total[4 * line + 2 * core + half].astype(jnp.bfloat16)
            give_ref[line, :, columns] = total[4 * line + 2 * (1 - core) + half].astype(jnp.bfloat16)


def local_product(parts, tiles, places, rows, core):
    own, below, above, beside = parts
    scalars = pl.BlockSpec(memory_space=pltpu.SMEM)
    whole = pl.BlockSpec(memory_space=pltpu.VMEM)
    sums = jax.ShapeDtypeStruct((BR + 1, NV, TB), jnp.float32)
    half_panel = jax.ShapeDtypeStruct((NY, NV, PIECE), jnp.bfloat16)
    params = pltpu.CompilerParams(vmem_limit_bytes=24 * 1024 * 1024)
    total = pl.pallas_call(
        early_kernel,
        out_shape=sums,
        in_specs=[scalars] * 2 + [whole] * 4,
        out_specs=whole,
        compiler_params=params,
        name="early_products",
    )(places, rows, own, above, beside, tiles)
    keep, give, _ = pl.pallas_call(
        late_kernel,
        out_shape=(half_panel, half_panel, sums),
        in_specs=[scalars] * 3 + [whole] * 3,
        out_specs=(whole,) * 3,
        input_output_aliases={3: 2},
        compiler_params=params,
        name="late_products",
    )(places, rows, core, total, below, tiles)
    return keep, give


def line_sum(keep, taken):
    pair = (keep.astype(jnp.float32) + taken.astype(jnp.float32)).astype(jnp.bfloat16)
    return jnp.sum(exchange(pair, LINES).astype(jnp.float32), axis=0)


def recurrence(sums, current, previous, center, half, step):
    shifted = (sums - center * current.astype(jnp.float32)) / half
    if step == 0:
        return shifted.astype(jnp.bfloat16)
    return (2.0 * shifted - previous.astype(jnp.float32)).astype(jnp.bfloat16)


def on_device(vectors, tiles, tile_row, tile_col, tile_count, lower, upper):
    center = (upper[0] + lower[0]) / 2.0
    half = (upper[0] - lower[0]) / 2.0
    row, col = lax.axis_index("row"), lax.axis_index("col")
    z, x, y, core = row // NX, row % NX, col // NC, col % NC
    places = block_places(tile_col, z, x, y, core)
    used = jnp.arange(SLOTS, dtype=jnp.int32) < tile_count[0]
    rows = jnp.where(used, tile_row, BR)
    core_ref = core.astype(jnp.int32)[None]
    current = previous = vectors
    moved = permute(current, to_column_plane)
    moved, tiles, places, rows, center, half = lax.optimization_barrier(
        (moved, load_tiles(tiles), places, rows, center, half)
    )
    for step in range(DEGREE):
        if step > 0:
            moved = permute(current, to_column_plane)
        parts = column_panel(moved)
        keep, give = local_product(parts, tiles, places, rows, core_ref)
        taken = permute(give, other_core)
        sums = line_sum(keep, taken)
        following = recurrence(sums, current, previous, center, half, step)
        previous, current = (current, following)
    return current


def solution(mesh):
    return jax.shard_map(
        on_device,
        mesh=mesh,
        in_specs=(
            P(None, AXES),
            P(AXES, None, None),
            P(AXES),
            P(AXES),
            P(AXES),
            P(),
            P(),
        ),
        out_specs=P(None, AXES),
        check_vma=False,
    )
```
